256 devices in a mesh: fsdp: 32 (over x, y, core), tensor: 8 (over z).
Axes of the slice: x: 4, y: 4, z: 8, core: 2. Of those that a mesh axis runs over, the one named last changes fastest.
Arguments:
- momentum: bfloat16 [8192, 26624], P('fsdp', 'tensor'), may hold values from -6 to 6
- gradient: bfloat16 [8192, 26624], P('fsdp', 'tensor'), may hold values from -6 to 6
- weight: bfloat16 [8192, 26624], P('fsdp', 'tensor'), may hold values from -6 to 6
- basis: bfloat16 [26624, 256], P('tensor'), may hold values from -0.0390625 to 0.0390625
Outputs:
- momentum_new: bfloat16 [8192, 26624], P('fsdp', 'tensor')
- weight_new: bfloat16 [8192, 26624], P('fsdp', 'tensor')
- basis_new: bfloat16 [26624, 256], P('tensor')
The draws below stay inside these ranges and needn't reach their ends.
All inputs are finite; a program needn't handle non-finite values.
Results may differ from the reference program's by a relative error of at most 0.0061.
Values may be sent and summed in bfloat16 or wider, within the bound.
No kernel may reach another device: no remote copies, remote signals or barrier semaphores. Data moves between devices by JAX's collectives and lax.ppermute only.
A program may use at most 64 MiB of HBM per device.

```python
import math
import jax
import jax.numpy as jnp
from jax import lax

D = 8192
FF = 26624
RANK = 256


def shard_levels(key, shape, cuts, least, high):
    def one(dim, parts):
        steps = jax.random.uniform(jax.random.fold_in(jax.random.fold_in(key, 6), dim), (parts,), jnp.float32, least / len(cuts), high / len(cuts))
        return jnp.repeat(jnp.exp(steps), shape[dim] // parts).reshape((-1,) + (1,) * (len(shape) - dim - 1))

    loudness = one(*cuts[0])
    for cut in cuts[1:]:
        loudness = loudness * one(*cut)
    return loudness


def gaussian(own_key, shape, width, bound, shards=(), held_as=jnp.bfloat16):
    drawn = width * jax.random.normal(own_key, shape, jnp.float32)
    if shards:
        drawn = drawn * shard_levels(own_key, shape, shards, -0.22, 0.18)
    return jnp.clip(drawn, -bound, bound).astype(held_as)


def setup_inputs(seed: int = 0) -> dict:
    seeds = jax.random.split(jax.random.key(seed), 5)
    momentum = gaussian(seeds[0], (D, FF), 1.0, 6.0, ((0, 32), (1, 8)))
    gradient = gaussian(seeds[1], (D, FF), 1.0, 6.0, ((0, 32), (1, 8)))
    weight = gaussian(seeds[2], (D, FF), 1.0, 6.0, ((0, 32), (1, 8)))
    basis = gaussian(seeds[3], (FF, RANK), FF ** -0.5, 0.0390625, ((0, 8),))
    return dict(momentum=momentum, gradient=gradient, weight=weight, basis=basis)


def reference(momentum, gradient, weight, basis):
    summed = momentum.astype(jnp.float32) + gradient.astype(jnp.float32)
    summed_b = summed.astype(jnp.bfloat16)
    proj = jnp.dot(summed_b.astype(jnp.float32), basis.astype(jnp.float32), preferred_element_type=jnp.float32)
    gram = jnp.dot(proj.T, proj, precision=lax.Precision.HIGHEST)
    lower = jnp.linalg.cholesky(gram)
    ortho = lax.linalg.triangular_solve(lower, proj, left_side=False, lower=True, transpose_a=True).astype(jnp.bfloat16)
    right = lax.dot_general(summed_b.astype(jnp.float32), ortho.astype(jnp.float32), (((0,), (0,)), ((), ())), preferred_element_type=jnp.float32)
    colsq = lax.optimization_barrier(jnp.sum(right * right, axis=0))
    basis_new = (right * lax.rsqrt(colsq + 1e-06)).astype(jnp.bfloat16)
    right_b = right.astype(jnp.bfloat16)
    back = lax.dot_general(ortho.astype(jnp.float32), right_b.astype(jnp.float32), (((1,), (1,)), ((), ())), preferred_element_type=jnp.float32)
    momentum_new = (summed - 0.05 * back).astype(jnp.bfloat16)
    update = lax.dot_general(ortho.astype(jnp.float32), basis_new.astype(jnp.float32), (((1,), (1,)), ((), ())), preferred_element_type=jnp.float32)
    factor = 0.2 * math.sqrt(D * FF / RANK)
    weight_new = (weight.astype(jnp.float32) - factor * update).astype(jnp.bfloat16)
    return (momentum_new, weight_new, basis_new)
```

```python
import math

import jax
import jax.numpy as jnp
from jax import lax
from jax.experimental import pallas as pl
from jax.experimental.pallas import tpu as pltpu
from jax.sharding import PartitionSpec as P

D = 8192
FF = 26624
RANK = 256
HALF = RANK // 2
F, T = "fsdp", "tensor"
HIGH = lax.Precision.HIGHEST
f32, bf16 = jnp.float32, jnp.bfloat16


def place(x, y, c):
    return ((x % 4) * 4 + y % 4) * 2 + c


def moves(fn):
    return [(place(x, y, c), place(*fn(x, y, c))) for x in range(4) for y in range(4) for c in range(2)]


CORE = moves(lambda x, y, c: (x, y, 1 - c))
YS = [moves(lambda x, y, c, k=k: (x, y + k, c)) for k in (1, 2, 3)]
XS = [moves(lambda x, y, c, k=k: (x + k, y, c)) for k in (1, 2, 3)]
ZS = [[(i, i ^ 1) for i in range(8)], [(i, i ^ 2) for i in range(8)], [(i, 7 - i) for i in range(8)]]
PLANE = [[place(x, y, c) for x in range(4) for y in range(4)] for c in range(2)]


def ring_sum(v, shifts):
    one, two, three = [lax.ppermute(v, F, s) for s in shifts]
    return (v + two) + (one + three)


def inverse_kernel(g_ref, w_ref, a_ref):
    n = RANK
    row = lax.broadcasted_iota(jnp.int32, (n, n), 0)
    col = lax.broadcasted_iota(jnp.int32, (n, n), 1)
    eye = row == col
    g = g_ref[...]
    on_diag = jnp.where(eye, g, 0.0)
    d_row = lax.rsqrt(jnp.sum(on_diag, axis=0, keepdims=True))
    d_col = lax.rsqrt(jnp.sum(on_diag, axis=1, keepdims=True))

    def correction(c):
        return jnp.where(row > col, c, 0.0) + jnp.where(eye, 0.5 * (c - 1.0), 0.0)

    ident = jnp.where(eye, 1.0, 0.0)
    w_ref[...] = (ident - correction(g * d_col * d_row)) * d_row

    def dot(a, b, dims):
        return lax.dot_general(a, b, (dims, ((), ())), precision=HIGH, preferred_element_type=f32)

    def step(state):
        k, _ = state
        w = w_ref[...]
        c = dot(dot(w, g_ref[...], ((1,), (0,))), w, ((1,), (1,)))
        off = c - ident
        w_ref[...] = w - dot(correction(c), w, ((1,), (0,)))
        return k + 1, jnp.sum(off * off)

    _, err = lax.while_loop(
        lambda s: jnp.logical_and(s[0] < 9, jnp.logical_not(s[1] < 1e-6)), step, (0, jnp.float32(1.0))
    )

    @pl.when(jnp.logical_not(err < 1e-6))
    def _():
        a_ref[...] = g_ref[...]
        w_ref[...] = ident

        def eliminate(j, carry):
            a_row = a_ref[pl.ds(j, 1), :]
            lane = lax.broadcasted_iota(jnp.int32, (1, n), 1)
            pivot = jnp.sum(jnp.where(lane == j, a_row, 0.0), axis=1, keepdims=True)
            a = a_ref[...]
            column = jnp.sum(jnp.where(col == j, a, 0.0), axis=1, keepdims=True)
            down = lax.broadcasted_iota(jnp.int32, (n, 1), 0)
            factor = jnp.where(down > j, column / pivot, 0.0)
            w_row = w_ref[pl.ds(j, 1), :]
            a_ref[...] = a - factor * a_row
            w_ref[...] = w_ref[...] - factor * w_row
            w_ref[pl.ds(j, 1), :] = w_row * lax.rsqrt(pivot)
            return carry

        lax.fori_loop(0, n, eliminate, 0)


def inverse_factor(gram):
    return pl.pallas_call(
        inverse_kernel,
        out_shape=jax.ShapeDtypeStruct((RANK, RANK), f32),
        scratch_shapes=[pltpu.VMEM((RANK, RANK), f32)],
        compiler_params=pltpu.CompilerParams(vmem_limit_bytes=16 * 1024 * 1024),
        name="inverse_factor",
    )(gram)


def local(momentum, gradient, weight, basis):
    core = lax.axis_index(F) % 2

    def join(own, other):
        return jnp.where(
            core == 0, jnp.concatenate([own, other], axis=-1), jnp.concatenate([other, own], axis=-1)
        )

    def share(v):
        return lax.dynamic_slice_in_dim(v, core * HALF, HALF, axis=-1)

    summed = momentum.astype(f32) + gradient.astype(f32)
    summed_b = summed.astype(bf16)
    summed_o = lax.ppermute(summed_b, F, CORE)

    part = jnp.dot(summed_b, basis, preferred_element_type=f32)
    rows = jnp.sum(lax.all_to_all(part.reshape(8, 32, RANK), T, 0, 0), axis=0)
    proj = lax.all_to_all(jnp.broadcast_to(rows, (8, 32, RANK)), T, 0, 0).reshape(256, RANK)
    proj_o = lax.ppermute(proj, F, CORE)

    both = jnp.concatenate([proj, proj_o], axis=0)
    mine = share(both)
    gram = lax.dot_general(mine, both, (((0,), (0,)), ((), ())), precision=HIGH, preferred_element_type=f32)
    gram = ring_sum(ring_sum(gram, YS), XS)
    gram_o = lax.ppermute(gram, F, CORE)
    gram = jnp.where(
        core == 0, jnp.concatenate([gram, gram_o], axis=0), jnp.concatenate([gram_o, gram], axis=0)
    )
    inv = inverse_factor(gram)

    high = mine.astype(bf16)
    low = (mine - high.astype(f32)).astype(bf16)
    split = jnp.concatenate([high, low], axis=1)
    over_rows = (((0,), (0,)), ((), ()))
    u = lax.dot_general(summed_b, split[:256], over_rows, preferred_element_type=f32) + lax.dot_general(
        summed_o, split[256:], over_rows, preferred_element_type=f32
    )
    u = u[:, :HALF] + u[:, HALF:]
    u = lax.all_to_all(u.reshape(16, 208, HALF), F, 0, 0, axis_index_groups=PLANE)
    u = jnp.sum(u, axis=0)
    u = join(u, lax.ppermute(u, F, CORE))

    over_rank = (((1,), (1,)), ((), ()))
    right = lax.dot_general(u, inv, over_rank, precision=HIGH, preferred_element_type=f32)
    ortho = lax.dot_general(proj, inv, over_rank, precision=HIGH, preferred_element_type=f32).astype(bf16)
    right = share(right).astype(bf16)
    right = lax.all_to_all(
        jnp.broadcast_to(right, (16, 208, HALF)), F, 0, 0, axis_index_groups=PLANE
    ).reshape(3328, HALF)
    right_b = join(right, lax.ppermute(right, F, CORE))
    wide = right_b.astype(f32)
    colsq = jnp.sum(wide * wide, axis=0, keepdims=True)
    for s in ZS:
        colsq = colsq + lax.ppermute(colsq, T, s)
    basis_new = (wide * lax.rsqrt(colsq + 1e-06)).astype(bf16)
    back = lax.dot_general(ortho, right_b, over_rank, preferred_element_type=f32)
    momentum_new = (summed - 0.05 * back).astype(bf16)
    update = lax.dot_general(ortho, basis_new, over_rank, preferred_element_type=f32)
    factor = 0.2 * math.sqrt(D * FF / RANK)
    weight_new = (weight.astype(f32) - factor * update).astype(bf16)
    return (momentum_new, weight_new, basis_new)


def solution(mesh):
    placed = (P(F, T), P(F, T), P(F, T), P(T, None))
    return jax.shard_map(
        local,
        mesh=mesh,
        in_specs=placed,
        out_specs=(P(F, T), P(F, T), P(T, None)),
        check_vma=False,
    )
```

```python
import math

import jax
import jax.numpy as jnp
from jax import lax
from jax.experimental import pallas as pl
from jax.experimental.pallas import tpu as pltpu
from jax.sharding import PartitionSpec as P

D = 8192
FF = 26624
RANK = 256
HALF = RANK // 2
F, T = "fsdp", "tensor"
HIGH = lax.Precision.HIGHEST
f32, bf16 = jnp.float32, jnp.bfloat16


def place(x, y, c):
    return ((x % 4) * 4 + y % 4) * 2 + c


def moves(fn):
    return [(place(x, y, c), place(*fn(x, y, c))) for x in range(4) for y in range(4) for c in range(2)]


CORE = moves(lambda x, y, c: (x, y, 1 - c))
YS = [moves(lambda x, y, c, k=k: (x, y + k, c)) for k in (1, 2, 3)]
XS = [moves(lambda x, y, c, k=k: (x + k, y, c)) for k in (1, 2, 3)]
ZS = [[(i, i ^ 1) for i in range(8)], [(i, i ^ 2) for i in range(8)], [(i, 7 - i) for i in range(8)]]
YG = [[place(x, y, c) for y in range(4)] for x in range(4) for c in range(2)]
XG = [[place(x, y, c) for x in range(4)] for y in range(4) for c in range(2)]
PLANE = [[place(x, y, c) for y in range(4) for x in range(4)] for c in range(2)]


def ring_sum(v, shifts):
    one, two, three = [lax.ppermute(v, F, s) for s in shifts]
    return (v + two) + (one + three)


def inverse_kernel(core_ref, own_ref, other_ref, w_ref, g_ref, a_ref):
    n = RANK
    first = core_ref[0] == 0
    g_ref[:HALF, :] = jnp.where(first, own_ref[...], other_ref[...])
    g_ref[HALF:, :] = jnp.where(first, other_ref[...], own_ref[...])
    row = lax.broadcasted_iota(jnp.int32, (n, n), 0)
    col = lax.broadcasted_iota(jnp.int32, (n, n), 1)
    eye = row == col
    g = g_ref[...]
    on_diag = jnp.where(eye, g, 0.0)
    d_row = lax.rsqrt(jnp.sum(on_diag, axis=0, keepdims=True))
    d_col = lax.rsqrt(jnp.sum(on_diag, axis=1, keepdims=True))

    def correction(c):
        return jnp.where(row > col, c, 0.0) + jnp.where(eye, 0.5 * (c - 1.0), 0.0)

    ident = jnp.where(eye, 1.0, 0.0)
    w_ref[...] = (ident - correction(g * d_col * d_row)) * d_row

    def dot(a, b, dims, precision=HIGH):
        return lax.dot_general(a, b, (dims, ((), ())), precision=precision, preferred_element_type=f32)

    def refine(precision):
        w = w_ref[...]
        c = dot(dot(w, g_ref[...], ((1,), (0,)), precision), w, ((1,), (1,)), precision)
        off = c - ident
        w_ref[...] = w - dot(correction(c), w, ((1,), (0,)), lax.Precision.DEFAULT)
        return jnp.sum(off * off)

    def step(state):
        return state[0] + 1, refine(HIGH)

    refine(lax.Precision.DEFAULT)

    _, err = lax.while_loop(
        lambda s: jnp.logical_and(s[0] < 10, jnp.logical_not(s[1] < 1e-6)), step, (0, jnp.float32(1.0))
    )

    @pl.when(jnp.logical_not(err < 1e-6))
    def _():
        a_ref[...] = g_ref[...]
        w_ref[...] = ident

        def eliminate(j, carry):
            a_row = a_ref[pl.ds(j, 1), :]
            lane = lax.broadcasted_iota(jnp.int32, (1, n), 1)
            pivot = jnp.sum(jnp.where(lane == j, a_row, 0.0), axis=1, keepdims=True)
            a = a_ref[...]
            column = jnp.sum(jnp.where(col == j, a, 0.0), axis=1, keepdims=True)
            down = lax.broadcasted_iota(jnp.int32, (n, 1), 0)
            factor = jnp.where(down > j, column / pivot, 0.0)
            w_row = w_ref[pl.ds(j, 1), :]
            a_ref[...] = a - factor * a_row
            w_ref[...] = w_ref[...] - factor * w_row
            w_ref[pl.ds(j, 1), :] = w_row * lax.rsqrt(pivot)
            return carry

        lax.fori_loop(0, n, eliminate, 0)


def inverse_factor(core, own, other):
    block = pl.BlockSpec(memory_space=pltpu.VMEM)
    return pl.pallas_call(
        inverse_kernel,
        out_shape=jax.ShapeDtypeStruct((RANK, RANK), f32),
        in_specs=[pl.BlockSpec(memory_space=pltpu.SMEM), block, block],
        out_specs=block,
        scratch_shapes=[pltpu.VMEM((RANK, RANK), f32)] * 2,
        compiler_params=pltpu.CompilerParams(vmem_limit_bytes=4 * 1024 * 1024),
        cost_estimate=pl.CostEstimate(flops=5_000_000_000, bytes_accessed=600_000, transcendentals=0),
        name="inverse_factor",
    )(core, own, other)


def assemble_kernel(place_ref, *refs):
    pieces, (split_ref, gram_ref, proj_ref, other_ref, sems) = refs[:8], refs[8:]
    first = place_ref[0] == 0
    order = place_ref[1]
    copies = []
    for n, piece in enumerate(pieces):
        at = pl.multiple_of(jnp.bitwise_xor(order, n % 4) * 64, 64)
        target = (proj_ref if n < 4 else other_ref).at[pl.ds(at, 64), :]
        copies.append(pltpu.make_async_copy(piece, target, sems.at[n]))
    for copy in copies:
        copy.start()
    for copy in copies:
        copy.wait()
    grams = []
    for at, ref in ((0, proj_ref), (256, other_ref)):
        whole = ref[...]
        mine = jnp.where(first, whole[:, :HALF], whole[:, HALF:])
        high = mine.astype(bf16)
        split_ref[at : at + 256, :HALF] = high
        split_ref[at : at + 256, HALF:] = (mine - high.astype(f32)).astype(bf16)
        grams.append(
            lax.dot_general(mine, whole, (((0,), (0,)), ((), ())), precision=HIGH, preferred_element_type=f32)
        )
    gram_ref[...] = grams[0] + grams[1]


def assemble(now, pieces):
    vmem = pl.BlockSpec(memory_space=pltpu.VMEM)
    return pl.pallas_call(
        assemble_kernel,
        in_specs=[pl.BlockSpec(memory_space=pltpu.SMEM)] + [pl.BlockSpec(memory_space=pl.ANY)] * 8,
        out_specs=[vmem] * 3,
        out_shape=[
            jax.ShapeDtypeStruct((512, RANK), bf16),
            jax.ShapeDtypeStruct((HALF, RANK), f32),
            jax.ShapeDtypeStruct((256, RANK), f32),
        ],
        scratch_shapes=[pltpu.VMEM((256, RANK), f32), pltpu.SemaphoreType.DMA((8,))],
        compiler_params=pltpu.CompilerParams(vmem_limit_bytes=4 * 1024 * 1024),
        cost_estimate=pl.CostEstimate(flops=200_000_000, bytes_accessed=1_200_000, transcendentals=0),
        name="assemble",
    )(now, *pieces)


def sum_over_z(part):
    z = lax.axis_index(T)
    label = jnp.where(z < 4, z, 7 - z)
    low, mid = label % 2, label // 2
    near = lambda v: lax.ppermute(v, T, ZS[0])
    next_ = lambda v: lax.ppermute(v, T, ZS[1])
    keep, send = low * 128 + mid * 64, low * 128 + (1 - mid) * 64
    got = near(lax.dynamic_slice_in_dim(part, (1 - low) * 128, 128, 0))
    out = lax.dynamic_slice_in_dim(part, send, 64, 0) + lax.dynamic_slice_in_dim(got, (1 - mid) * 64, 64, 0)
    kept = lax.dynamic_slice_in_dim(part, keep, 64, 0) + lax.dynamic_slice_in_dim(got, mid * 64, 64, 0)
    kept = kept + next_(out)
    a = kept + lax.ppermute(kept, T, ZS[2])
    b, c = next_(a), near(a)
    d = near(b)
    return (a, b, c, d), low * 2 + mid


def local(momentum, gradient, weight, basis):
    core = lax.axis_index(F) % 2

    def join(own, other):
        return jnp.where(
            core == 0, jnp.concatenate([own, other], axis=-1), jnp.concatenate([other, own], axis=-1)
        )

    def share(v):
        return lax.dynamic_slice_in_dim(v, core * HALF, HALF, axis=-1)

    summed = momentum.astype(f32) + gradient.astype(f32)
    summed_b = summed.astype(bf16)
    part = jnp.dot(summed_b, basis, preferred_element_type=f32)
    part, m2, g2 = lax.optimization_barrier((part, momentum, gradient))
    summed_b = (m2.astype(f32) + g2.astype(f32)).astype(bf16)
    summed_o = lax.ppermute(summed_b, F, CORE)
    pieces, order = sum_over_z(part)
    others = [lax.ppermute(p, F, CORE) for p in pieces]
    place_x, place_y = lax.axis_index(F) // 8, lax.axis_index(F) // 2 % 4

    now = jnp.stack([core, order]).astype(jnp.int32)
    split, gram, proj = assemble(now, [*pieces, *others])
    over_rows = (((0,), (0,)), ((), ()))
    u = lax.dot_general(summed_b, split[:256], over_rows, preferred_element_type=f32) + lax.dot_general(
        summed_o, split[256:], over_rows, preferred_element_type=f32
    )

    def along(v, k, here, size):
        return lax.dynamic_slice_in_dim(v, (here + k) % 4 * size, size, 0)

    us = []
    for k in range(4):
        w = along(u, k, place_y, 832)
        us.append(w[:, :HALF] + w[:, HALF:])
    us = [us[0]] + [lax.ppermute(us[k], F, YS[k - 1]) for k in (1, 2, 3)]
    gram = ring_sum(gram, XS)
    gram, us[0] = lax.optimization_barrier((gram, us[0]))
    gram = ring_sum(gram, YS)
    vs = []
    for k in range(4):
        w = [along(v, k, place_x, 208) for v in us]
        vs.append((w[0] + w[2]) + (w[1] + w[3]))
    u = vs[0] + lax.ppermute(vs[2], F, XS[1])
    u = u + (lax.ppermute(vs[1], F, XS[0]) + lax.ppermute(vs[3], F, XS[2]))
    inv = inverse_factor(now, gram, lax.ppermute(gram, F, CORE))
    u = join(u, lax.ppermute(u, F, CORE))

    over_rank = (((1,), (1,)), ((), ()))
    right = lax.dot_general(u, inv, over_rank, precision=HIGH, preferred_element_type=f32)
    ortho = lax.dot_general(proj, inv, over_rank, precision=HIGH, preferred_element_type=f32).astype(bf16)
    right = share(right).astype(bf16)
    right = lax.all_to_all(
        jnp.broadcast_to(right, (16, 208, HALF)), F, 0, 0, axis_index_groups=PLANE
    ).reshape(3328, HALF)
    right_b = join(right, lax.ppermute(right, F, CORE))
    back = lax.dot_general(ortho, right_b, over_rank, preferred_element_type=f32)
    momentum_new = (summed - 0.05 * back).astype(bf16)
    colsq = jnp.sum(jnp.square(right.astype(f32)), axis=0, keepdims=True)
    for i, s in enumerate(ZS):
        got = lax.ppermute(colsq, T, s)
        if i == 2:
            got, momentum_new = lax.optimization_barrier((got, momentum_new))
        colsq = colsq + got
    colsq = join(colsq, lax.ppermute(colsq, F, CORE))
    basis_new = (right_b.astype(f32) * lax.rsqrt(colsq + 1e-06)).astype(bf16)
    update = lax.dot_general(ortho, basis_new, over_rank, preferred_element_type=f32)
    factor = 0.2 * math.sqrt(D * FF / RANK)
    weight_new = (weight.astype(f32) - factor * update).astype(bf16)
    return (momentum_new, weight_new, basis_new)


def solution(mesh):
    placed = (P(F, T), P(F, T), P(F, T), P(T, None))
    return jax.shard_map(
        local,
        mesh=mesh,
        in_specs=placed,
        out_specs=(P(F, T), P(F, T), P(T, None)),
        check_vma=False,
    )
```

```python
import math

import jax
import jax.numpy as jnp
from jax import lax
from jax.experimental import pallas as pl
from jax.experimental.pallas import tpu as pltpu
from jax.sharding import PartitionSpec as P

D = 8192
FF = 26624
RANK = 256
HALF = RANK // 2
F, T = "fsdp", "tensor"
HIGH = lax.Precision.HIGHEST
f32, bf16 = jnp.float32, jnp.bfloat16


def place(x, y, c):
    return ((x % 4) * 4 + y % 4) * 2 + c


def moves(fn):
    return [(place(x, y, c), place(*fn(x, y, c))) for x in range(4) for y in range(4) for c in range(2)]


CORE = moves(lambda x, y, c: (x, y, 1 - c))
YS = [moves(lambda x, y, c, k=k: (x, y + k, c)) for k in (1, 2, 3)]
XS = [moves(lambda x, y, c, k=k: (x + k, y, c)) for k in (1, 2, 3)]
ZS = [[(i, i ^ 1) for i in range(8)], [(i, i ^ 2) for i in range(8)], [(i, 7 - i) for i in range(8)]]
YG = [[place(x, y, c) for y in range(4)] for x in range(4) for c in range(2)]
XG = [[place(x, y, c) for x in range(4)] for y in range(4) for c in range(2)]
PLANE = [[place(x, y, c) for y in range(4) for x in range(4)] for c in range(2)]


def ring_sum(v, shifts):
    one, two, three = [lax.ppermute(v, F, s) for s in shifts]
    return (v + two) + (one + three)


def inverse_kernel(core_ref, own_ref, other_ref, w_ref, g_ref, a_ref):
    n = RANK
    first = core_ref[0] == 0
    g_ref[:HALF, :] = jnp.where(first, own_ref[...], other_ref[...])
    g_ref[HALF:, :] = jnp.where(first, other_ref[...], own_ref[...])
    row = lax.broadcasted_iota(jnp.int32, (n, n), 0)
    col = lax.broadcasted_iota(jnp.int32, (n, n), 1)
    eye = row == col
    g = g_ref[...]
    on_diag = jnp.where(eye, g, 0.0)
    d_row = lax.rsqrt(jnp.sum(on_diag, axis=0, keepdims=True))
    d_col = lax.rsqrt(jnp.sum(on_diag, axis=1, keepdims=True))

    def correction(c):
        return jnp.where(row > col, c, 0.0) + jnp.where(eye, 0.5 * (c - 1.0), 0.0)

    ident = jnp.where(eye, 1.0, 0.0)
    w_ref[...] = (ident - correction(g * d_col * d_row)) * d_row

    def dot(a, b, dims, precision=HIGH):
        return lax.dot_general(a, b, (dims, ((), ())), precision=precision, preferred_element_type=f32)

    def refine(precision):
        w = w_ref[...]
        c = dot(dot(w, g_ref[...], ((1,), (0,)), precision), w, ((1,), (1,)), precision)
        off = c - ident
        w_ref[...] = w - dot(correction(c), w, ((1,), (0,)), lax.Precision.DEFAULT)
        return jnp.sum(off * off)

    def step(state):
        return state[0] + 1, refine(HIGH)

    refine(lax.Precision.DEFAULT)

    _, err = lax.while_loop(
        lambda s: jnp.logical_and(s[0] < 10, jnp.logical_not(s[1] < 1e-6)), step, (0, jnp.float32(1.0))
    )

    @pl.when(jnp.logical_not(err < 1e-6))
    def _():
        a_ref[...] = g_ref[...]
        w_ref[...] = ident

        def eliminate(j, carry):
            a_row = a_ref[pl.ds(j, 1), :]
            lane = lax.broadcasted_iota(jnp.int32, (1, n), 1)
            pivot = jnp.sum(jnp.where(lane == j, a_row, 0.0), axis=1, keepdims=True)
            a = a_ref[...]
            column = jnp.sum(jnp.where(col == j, a, 0.0), axis=1, keepdims=True)
            down = lax.broadcasted_iota(jnp.int32, (n, 1), 0)
            factor = jnp.where(down > j, column / pivot, 0.0)
            w_row = w_ref[pl.ds(j, 1), :]
            a_ref[...] = a - factor * a_row
            w_ref[...] = w_ref[...] - factor * w_row
            w_ref[pl.ds(j, 1), :] = w_row * lax.rsqrt(pivot)
            return carry

        lax.fori_loop(0, n, eliminate, 0)


def inverse_factor(core, own, other):
    block = pl.BlockSpec(memory_space=pltpu.VMEM)
    return pl.pallas_call(
        inverse_kernel,
        out_shape=jax.ShapeDtypeStruct((RANK, RANK), f32),
        in_specs=[pl.BlockSpec(memory_space=pltpu.SMEM), block, block],
        out_specs=block,
        scratch_shapes=[pltpu.VMEM((RANK, RANK), f32)] * 2,
        compiler_params=pltpu.CompilerParams(vmem_limit_bytes=4 * 1024 * 1024),
        cost_estimate=pl.CostEstimate(flops=5_000_000_000, bytes_accessed=600_000, transcendentals=0),
        name="inverse_factor",
    )(core, own, other)


WIDE = 1664


def project_kernel(m_ref, g_ref, basis_ref, s_ref, part_ref):
    s = (m_ref[...].astype(f32) + g_ref[...].astype(f32)).astype(bf16)
    s_ref[...] = s
    part = jnp.dot(s, basis_ref[...], preferred_element_type=f32)

    @pl.when(pl.program_id(0) == 0)
    def _():
        part_ref[...] = part

    @pl.when(pl.program_id(0) > 0)
    def _():
        part_ref[...] += part


def project(momentum, gradient, basis):
    columns = pl.BlockSpec((256, WIDE), lambda i: (0, i))
    return pl.pallas_call(
        project_kernel,
        grid=(2,),
        in_specs=[columns, columns, pl.BlockSpec((WIDE, RANK), lambda i: (i, 0))],
        out_specs=[columns, pl.BlockSpec((256, RANK), lambda i: (0, 0))],
        out_shape=[
            jax.ShapeDtypeStruct((256, 3328), bf16),
            jax.ShapeDtypeStruct((256, RANK), f32),
        ],
        compiler_params=pltpu.CompilerParams(vmem_limit_bytes=24 * 1024 * 1024),
        cost_estimate=pl.CostEstimate(flops=440_000_000, bytes_accessed=7_000_000, transcendentals=0),
        name="project",
    )(momentum, gradient, basis)


def spread_kernel(place_ref, s_ref, so_ref, *refs):
    pieces, refs = refs[:8], refs[8:]
    outs, (gram_ref, proj_ref, other_ref, split_ref, sems) = refs[:4], refs[4:]
    step = pl.program_id(0)

    @pl.when(step == 0)
    def _():
        first = place_ref[0] == 0
        order = place_ref[1]
        copies = []
        for n, piece in enumerate(pieces):
            at = pl.multiple_of(jnp.bitwise_xor(order, n % 4) * 64, 64)
            target = (proj_ref if n < 4 else other_ref).at[pl.ds(at, 64), :]
            copies.append(pltpu.make_async_copy(piece, target, sems.at[n]))
        for copy in copies:
            copy.start()
        for copy in copies:
            copy.wait()
        grams = []
        for at, ref in ((0, proj_ref), (256, other_ref)):
            whole = ref[...]
            mine = jnp.where(first, whole[:, :HALF], whole[:, HALF:])
            turned = mine.T
            high = turned.astype(bf16)
            split_ref[:HALF, at : at + 256] = high
            split_ref[HALF:, at : at + 256] = (turned - high.astype(f32)).astype(bf16)
            grams.append(jnp.dot(turned, whole, precision=HIGH, preferred_element_type=f32))
        gram_ref[...] = grams[0] + grams[1]

    u = jnp.dot(split_ref[:, :256], s_ref[...], preferred_element_type=f32)
    u = u + jnp.dot(split_ref[:, 256:], so_ref[...], preferred_element_type=f32)
    u = (u[:HALF, :] + u[HALF:, :]).T
    for j in range(2):
        ahead = jnp.bitwise_and(step * 2 + j + 4 - place_ref[2], 3)
        for k in range(4):

            @pl.when(ahead == k)
            def _():
                outs[k][...] = u[j * 832 : (j + 1) * 832, :]


def spread(now, summed_b, summed_o, pieces):
    columns = pl.BlockSpec((256, WIDE), lambda i, p: (0, i))
    whole = lambda *shape: pl.BlockSpec(shape, lambda i, p: (0, 0))
    return pl.pallas_call(
        spread_kernel,
        grid_spec=pltpu.PrefetchScalarGridSpec(
            num_scalar_prefetch=1,
            grid=(2,),
            in_specs=[columns, columns] + [pl.BlockSpec(memory_space=pl.ANY)] * 8,
            out_specs=[whole(832, HALF)] * 4 + [whole(HALF, RANK), whole(256, RANK)],
            scratch_shapes=[
                pltpu.VMEM((256, RANK), f32),
                pltpu.VMEM((RANK, 512), bf16),
                pltpu.SemaphoreType.DMA((8,)),
            ],
        ),
        out_shape=[jax.ShapeDtypeStruct((832, HALF), f32)] * 4
        + [jax.ShapeDtypeStruct((HALF, RANK), f32), jax.ShapeDtypeStruct((256, RANK), f32)],
        compiler_params=pltpu.CompilerParams(vmem_limit_bytes=32 * 1024 * 1024),
        cost_estimate=pl.CostEstimate(flops=2_000_000_000, bytes_accessed=6_000_000, transcendentals=0),
        name="spread",
    )(now, summed_b, summed_o, *pieces)


def sum_over_z(part):
    z = lax.axis_index(T)
    label = jnp.where(z < 4, z, 7 - z)
    low, mid = label % 2, label // 2
    near = lambda v: lax.ppermute(v, T, ZS[0])
    next_ = lambda v: lax.ppermute(v, T, ZS[1])
    keep, send = low * 128 + mid * 64, low * 128 + (1 - mid) * 64
    got = near(lax.dynamic_slice_in_dim(part, (1 - low) * 128, 128, 0))
    out = lax.dynamic_slice_in_dim(part, send, 64, 0) + lax.dynamic_slice_in_dim(got, (1 - mid) * 64, 64, 0)
    kept = lax.dynamic_slice_in_dim(part, keep, 64, 0) + lax.dynamic_slice_in_dim(got, mid * 64, 64, 0)
    kept = kept + next_(out)
    a = kept + lax.ppermute(kept, T, ZS[2])
    b, c = next_(a), near(a)
    d = near(b)
    return (a, b, c, d), low * 2 + mid


def local(momentum, gradient, weight, basis):
    core = lax.axis_index(F) % 2

    def join(own, other):
        return jnp.where(
            core == 0, jnp.concatenate([own, other], axis=-1), jnp.concatenate([other, own], axis=-1)
        )

    def share(v):
        return lax.dynamic_slice_in_dim(v, core * HALF, HALF, axis=-1)

    summed = momentum.astype(f32) + gradient.astype(f32)
    summed_b, part = project(momentum, gradient, basis)
    summed_o = lax.ppermute(summed_b, F, CORE)
    pieces, order = sum_over_z(part)
    others = [lax.ppermute(p, F, CORE) for p in pieces]
    place_x, place_y = lax.axis_index(F) // 8, lax.axis_index(F) // 2 % 4
    now = jnp.stack([core, order, place_y]).astype(jnp.int32)
    *us, gram, proj = spread(now, summed_b, summed_o, [*pieces, *others])

    def along(v, k, here, size):
        return lax.dynamic_slice_in_dim(v, (here + k) % 4 * size, size, 0)

    us = [us[0]] + [lax.ppermute(us[k], F, YS[k - 1]) for k in (1, 2, 3)]
    gram = ring_sum(gram, XS)
    gram, us[0] = lax.optimization_barrier((gram, us[0]))
    gram = ring_sum(gram, YS)
    vs = []
    for k in range(4):
        w = [along(v, k, place_x, 208) for v in us]
        vs.append((w[0] + w[2]) + (w[1] + w[3]))
    u = vs[0] + lax.ppermute(vs[2], F, XS[1])
    u = u + (lax.ppermute(vs[1], F, XS[0]) + lax.ppermute(vs[3], F, XS[2]))
    inv = inverse_factor(now, gram, lax.ppermute(gram, F, CORE))
    u = join(u, lax.ppermute(u, F, CORE))

    over_rank = (((1,), (1,)), ((), ()))
    right = lax.dot_general(u, inv, over_rank, precision=HIGH, preferred_element_type=f32)
    ortho = lax.dot_general(proj, inv, over_rank, precision=HIGH, preferred_element_type=f32).astype(bf16)
    right = share(right).astype(bf16)
    right = lax.all_to_all(
        jnp.broadcast_to(right, (16, 208, HALF)), F, 0, 0, axis_index_groups=PLANE
    ).reshape(3328, HALF)
    right_b = join(right, lax.ppermute(right, F, CORE))
    back = lax.dot_general(ortho, right_b, over_rank, preferred_element_type=f32)
    momentum_new = (summed - 0.05 * back).astype(bf16)
    colsq = jnp.sum(jnp.square(right.astype(f32)), axis=0, keepdims=True)
    for i, s in enumerate(ZS):
        got = lax.ppermute(colsq, T, s)
        if i == 2:
            got, momentum_new = lax.optimization_barrier((got, momentum_new))
        colsq = colsq + got
    colsq = join(colsq, lax.ppermute(colsq, F, CORE))
    basis_new = (right_b.astype(f32) * lax.rsqrt(colsq + 1e-06)).astype(bf16)
    update = lax.dot_general(ortho, basis_new, over_rank, preferred_element_type=f32)
    factor = 0.2 * math.sqrt(D * FF / RANK)
    weight_new = (weight.astype(f32) - factor * update).astype(bf16)
    return (momentum_new, weight_new, basis_new)


def solution(mesh):
    placed = (P(F, T), P(F, T), P(F, T), P(T, None))
    return jax.shard_map(
        local,
        mesh=mesh,
        in_specs=placed,
        out_specs=(P(F, T), P(F, T), P(T, None)),
        check_vma=False,
    )
```

```python
import math

import jax
import jax.numpy as jnp
from jax import lax
from jax.experimental import pallas as pl
from jax.experimental.pallas import tpu as pltpu
from jax.sharding import PartitionSpec as P

D = 8192
FF = 26624
RANK = 256
HALF = RANK // 2
F, T = "fsdp", "tensor"
HIGH = lax.Precision.HIGHEST
f32, bf16 = jnp.float32, jnp.bfloat16


def place(x, y, c):
    return ((x % 4) * 4 + y % 4) * 2 + c


def moves(fn):
    return [(place(x, y, c), place(*fn(x, y, c))) for x in range(4) for y in range(4) for c in range(2)]


CORE = moves(lambda x, y, c: (x, y, 1 - c))
YS = [moves(lambda x, y, c, k=k: (x, y + k, c)) for k in (1, 2, 3)]
XS = [moves(lambda x, y, c, k=k: (x + k, y, c)) for k in (1, 2, 3)]
ZS = [[(i, i ^ 1) for i in range(8)], [(i, i ^ 2) for i in range(8)], [(i, 7 - i) for i in range(8)]]
YG = [[place(x, y, c) for y in range(4)] for x in range(4) for c in range(2)]
XG = [[place(x, y, c) for x in range(4)] for y in range(4) for c in range(2)]
PLANE = [[place(x, y, c) for y in range(4) for x in range(4)] for c in range(2)]


def ring_sum(v, shifts):
    one, two, three = [lax.ppermute(v, F, s) for s in shifts]
    return (v + two) + (one + three)


def inverse_kernel(core_ref, own_ref, other_ref, w_ref, g_ref, a_ref):
    n = RANK
    first = core_ref[0] == 0
    g_ref[:HALF, :] = jnp.where(first, own_ref[...], other_ref[...])
    g_ref[HALF:, :] = jnp.where(first, other_ref[...], own_ref[...])
    row = lax.broadcasted_iota(jnp.int32, (n, n), 0)
    col = lax.broadcasted_iota(jnp.int32, (n, n), 1)
    eye = row == col
    g = g_ref[...]
    on_diag = jnp.where(eye, g, 0.0)
    d_row = lax.rsqrt(jnp.sum(on_diag, axis=0, keepdims=True))
    d_col = lax.rsqrt(jnp.sum(on_diag, axis=1, keepdims=True))

    def correction(c):
        return jnp.where(row > col, c, 0.0) + jnp.where(eye, 0.5 * (c - 1.0), 0.0)

    ident = jnp.where(eye, 1.0, 0.0)
    w_ref[...] = (ident - correction(g * d_col * d_row)) * d_row

    def dot(a, b, dims, precision=HIGH):
        return lax.dot_general(a, b, (dims, ((), ())), precision=precision, preferred_element_type=f32)

    def refine(precision):
        w = w_ref[...]
        c = dot(dot(w, g_ref[...], ((1,), (0,)), precision), w, ((1,), (1,)), precision)
        off = c - ident
        w_ref[...] = w - dot(correction(c), w, ((1,), (0,)), lax.Precision.DEFAULT)
        return jnp.sum(off * off)

    def step(state):
        return state[0] + 1, refine(HIGH)

    refine(lax.Precision.DEFAULT)

    _, err = lax.while_loop(
        lambda s: jnp.logical_and(s[0] < 10, jnp.logical_not(s[1] < 1e-6)), step, (0, jnp.float32(1.0))
    )

    @pl.when(jnp.logical_not(err < 1e-6))
    def _():
        a_ref[...] = g_ref[...]
        w_ref[...] = ident

        def eliminate(j, carry):
            a_row = a_ref[pl.ds(j, 1), :]
            lane = lax.broadcasted_iota(jnp.int32, (1, n), 1)
            pivot = jnp.sum(jnp.where(lane == j, a_row, 0.0), axis=1, keepdims=True)
            a = a_ref[...]
            column = jnp.sum(jnp.where(col == j, a, 0.0), axis=1, keepdims=True)
            down = lax.broadcasted_iota(jnp.int32, (n, 1), 0)
            factor = jnp.where(down > j, column / pivot, 0.0)
            w_row = w_ref[pl.ds(j, 1), :]
            a_ref[...] = a - factor * a_row
            w_ref[...] = w_ref[...] - factor * w_row
            w_ref[pl.ds(j, 1), :] = w_row * lax.rsqrt(pivot)
            return carry

        lax.fori_loop(0, n, eliminate, 0)


def inverse_factor(core, own, other):
    block = pl.BlockSpec(memory_space=pltpu.VMEM)
    return pl.pallas_call(
        inverse_kernel,
        out_shape=jax.ShapeDtypeStruct((RANK, RANK), f32),
        in_specs=[pl.BlockSpec(memory_space=pltpu.SMEM), block, block],
        out_specs=block,
        scratch_shapes=[pltpu.VMEM((RANK, RANK), f32)] * 2,
        compiler_params=pltpu.CompilerParams(vmem_limit_bytes=4 * 1024 * 1024),
        cost_estimate=pl.CostEstimate(flops=5_000_000_000, bytes_accessed=600_000, transcendentals=0),
        name="inverse_factor",
    )(core, own, other)


WIDE = 1664


def project_kernel(m_ref, g_ref, basis_ref, s_ref, part_ref):
    s = (m_ref[...].astype(f32) + g_ref[...].astype(f32)).astype(bf16)
    s_ref[...] = s
    part = jnp.dot(s, basis_ref[...], preferred_element_type=f32)

    @pl.when(pl.program_id(0) == 0)
    def _():
        part_ref[...] = part

    @pl.when(pl.program_id(0) > 0)
    def _():
        part_ref[...] += part


def project(momentum, gradient, basis):
    columns = pl.BlockSpec((256, WIDE), lambda i: (0, i))
    return pl.pallas_call(
        project_kernel,
        grid=(2,),
        in_specs=[columns, columns, pl.BlockSpec((WIDE, RANK), lambda i: (i, 0))],
        out_specs=[columns, pl.BlockSpec((256, RANK), lambda i: (0, 0))],
        out_shape=[
            jax.ShapeDtypeStruct((256, 3328), bf16),
            jax.ShapeDtypeStruct((256, RANK), f32),
        ],
        compiler_params=pltpu.CompilerParams(vmem_limit_bytes=24 * 1024 * 1024),
        cost_estimate=pl.CostEstimate(flops=440_000_000, bytes_accessed=7_000_000, transcendentals=0),
        name="project",
    )(momentum, gradient, basis)


def spread_kernel(place_ref, s_ref, so_ref, *refs):
    pieces, refs = refs[:8], refs[8:]
    outs, (gram_ref, proj_ref, other_ref, split_ref, sems) = refs[:4], refs[4:]
    step = pl.program_id(0)

    @pl.when(step == 0)
    def _():
        first = place_ref[0] == 0
        order = place_ref[1]
        copies = []
        for n, piece in enumerate(pieces):
            at = pl.multiple_of(jnp.bitwise_xor(order, n % 4) * 64, 64)
            target = (proj_ref if n < 4 else other_ref).at[pl.ds(at, 64), :]
            copies.append(pltpu.make_async_copy(piece, target, sems.at[n]))
        for copy in copies:
            copy.start()
        for copy in copies:
            copy.wait()
        grams = []
        for at, ref in ((0, proj_ref), (256, other_ref)):
            whole = ref[...]
            mine = jnp.where(first, whole[:, :HALF], whole[:, HALF:])
            turned = mine.T
            high = turned.astype(bf16)
            split_ref[:HALF, at : at + 256] = high
            split_ref[HALF:, at : at + 256] = (turned - high.astype(f32)).astype(bf16)
            grams.append(jnp.dot(turned, whole, precision=HIGH, preferred_element_type=f32))
        gram_ref[...] = grams[0] + grams[1]

    u = jnp.dot(split_ref[:, :256], s_ref[...], preferred_element_type=f32)
    u = u + jnp.dot(split_ref[:, 256:], so_ref[...], preferred_element_type=f32)
    u = (u[:HALF, :] + u[HALF:, :]).T
    for j in range(2):
        ahead = jnp.bitwise_and(step * 2 + j + 4 - place_ref[2], 3)
        for k in range(4):

            @pl.when(ahead == k)
            def _():
                outs[k][...] = u[j * 832 : (j + 1) * 832, :]


def spread(now, summed_b, summed_o, pieces):
    columns = pl.BlockSpec((256, WIDE), lambda i, p: (0, i))
    whole = lambda *shape: pl.BlockSpec(shape, lambda i, p: (0, 0))
    return pl.pallas_call(
        spread_kernel,
        grid_spec=pltpu.PrefetchScalarGridSpec(
            num_scalar_prefetch=1,
            grid=(2,),
            in_specs=[columns, columns] + [pl.BlockSpec(memory_space=pl.ANY)] * 8,
            out_specs=[whole(832, HALF)] * 4 + [whole(HALF, RANK), whole(256, RANK)],
            scratch_shapes=[
                pltpu.VMEM((256, RANK), f32),
                pltpu.VMEM((RANK, 512), bf16),
                pltpu.SemaphoreType.DMA((8,)),
            ],
        ),
        out_shape=[jax.ShapeDtypeStruct((832, HALF), f32)] * 4
        + [jax.ShapeDtypeStruct((HALF, RANK), f32), jax.ShapeDtypeStruct((256, RANK), f32)],
        compiler_params=pltpu.CompilerParams(vmem_limit_bytes=32 * 1024 * 1024),
        cost_estimate=pl.CostEstimate(flops=2_000_000_000, bytes_accessed=6_000_000, transcendentals=0),
        name="spread",
    )(now, summed_b, summed_o, *pieces)


FACTOR = 0.2 * math.sqrt(D * FF / RANK)


def finish_kernel(place_ref, own_ref, other_ref, colsq_ref, ortho_ref, weight_ref, basis_ref, out_ref):
    first = place_ref[0] == 0
    own, other = own_ref[...].astype(f32), other_ref[...].astype(f32)
    right = jnp.concatenate([jnp.where(first, own, other), jnp.where(first, other, own)], axis=1)
    basis = (right * lax.rsqrt(colsq_ref[...] + 1e-06)).astype(bf16)
    basis_ref[...] = basis
    update = lax.dot_general(
        ortho_ref[...], basis, (((1,), (1,)), ((), ())), preferred_element_type=f32
    )
    out_ref[...] = (weight_ref[...].astype(f32) - FACTOR * update).astype(bf16)


def finish(now, own, other, colsq, ortho, weight):
    columns = pl.BlockSpec((256, WIDE), lambda i, p: (0, i))
    half = pl.BlockSpec((WIDE, HALF), lambda i, p: (i, 0))
    return pl.pallas_call(
        finish_kernel,
        grid_spec=pltpu.PrefetchScalarGridSpec(
            num_scalar_prefetch=1,
            grid=(2,),
            in_specs=[
                half,
                half,
                pl.BlockSpec((1, RANK), lambda i, p: (0, 0)),
                pl.BlockSpec((256, RANK), lambda i, p: (0, 0)),
                columns,
            ],
            out_specs=[pl.BlockSpec((WIDE, RANK), lambda i, p: (i, 0)), columns],
        ),
        out_shape=[
            jax.ShapeDtypeStruct((3328, RANK), bf16),
            jax.ShapeDtypeStruct((256, 3328), bf16),
        ],
        compiler_params=pltpu.CompilerParams(vmem_limit_bytes=24 * 1024 * 1024),
        cost_estimate=pl.CostEstimate(flops=440_000_000, bytes_accessed=7_000_000, transcendentals=0),
        name="finish",
    )(now, own, other, colsq, ortho, weight)


def sum_over_z(part):
    z = lax.axis_index(T)
    label = jnp.where(z < 4, z, 7 - z)
    low, mid = label % 2, label // 2
    near = lambda v: lax.ppermute(v, T, ZS[0])
    next_ = lambda v: lax.ppermute(v, T, ZS[1])
    keep, send = low * 128 + mid * 64, low * 128 + (1 - mid) * 64
    got = near(lax.dynamic_slice_in_dim(part, (1 - low) * 128, 128, 0))
    out = lax.dynamic_slice_in_dim(part, send, 64, 0) + lax.dynamic_slice_in_dim(got, (1 - mid) * 64, 64, 0)
    kept = lax.dynamic_slice_in_dim(part, keep, 64, 0) + lax.dynamic_slice_in_dim(got, mid * 64, 64, 0)
    kept = kept + next_(out)
    a = kept + lax.ppermute(kept, T, ZS[2])
    b, c = next_(a), near(a)
    d = near(b)
    return (a, b, c, d), low * 2 + mid


def local(momentum, gradient, weight, basis):
    core = lax.axis_index(F) % 2

    def join(own, other):
        return jnp.where(
            core == 0, jnp.concatenate([own, other], axis=-1), jnp.concatenate([other, own], axis=-1)
        )

    def share(v):
        return lax.dynamic_slice_in_dim(v, core * HALF, HALF, axis=-1)

    summed = momentum.astype(f32) + gradient.astype(f32)
    summed_b, part = project(momentum, gradient, basis)
    summed_o = lax.ppermute(summed_b, F, CORE)
    pieces, order = sum_over_z(part)
    others = [lax.ppermute(p, F, CORE) for p in pieces]
    place_x, place_y = lax.axis_index(F) // 8, lax.axis_index(F) // 2 % 4
    now = jnp.stack([core, order, place_y]).astype(jnp.int32)
    *us, gram, proj = spread(now, summed_b, summed_o, [*pieces, *others])

    def along(v, k, here, size):
        return lax.dynamic_slice_in_dim(v, (here + k) % 4 * size, size, 0)

    us = [us[0]] + [lax.ppermute(us[k], F, YS[k - 1]) for k in (1, 2, 3)]
    gram = ring_sum(gram, XS)
    gram, us[0] = lax.optimization_barrier((gram, us[0]))
    gram = ring_sum(gram, YS)
    vs = []
    for k in range(4):
        w = [along(v, k, place_x, 208) for v in us]
        vs.append((w[0] + w[2]) + (w[1] + w[3]))
    u = vs[0] + lax.ppermute(vs[2], F, XS[1])
    u = u + (lax.ppermute(vs[1], F, XS[0]) + lax.ppermute(vs[3], F, XS[2]))
    inv = inverse_factor(now, gram, lax.ppermute(gram, F, CORE))
    u = join(u, lax.ppermute(u, F, CORE))

    over_rank = (((1,), (1,)), ((), ()))
    right = lax.dot_general(u, inv, over_rank, precision=HIGH, preferred_element_type=f32)
    ortho = lax.dot_general(proj, inv, over_rank, precision=HIGH, preferred_element_type=f32).astype(bf16)
    right = share(right).astype(bf16)
    right = lax.all_to_all(
        jnp.broadcast_to(right, (16, 208, HALF)), F, 0, 0, axis_index_groups=PLANE
    ).reshape(3328, HALF)
    right_o = lax.ppermute(right, F, CORE)
    right_b = join(right, right_o)
    back = lax.dot_general(ortho, right_b, over_rank, preferred_element_type=f32)
    momentum_new = (summed - 0.05 * back).astype(bf16)
    colsq = jnp.sum(jnp.square(right.astype(f32)), axis=0, keepdims=True)
    for i, s in enumerate(ZS):
        got = lax.ppermute(colsq, T, s)
        if i == 2:
            got, momentum_new = lax.optimization_barrier((got, momentum_new))
        colsq = colsq + got
    colsq = join(colsq, lax.ppermute(colsq, F, CORE))
    basis_new, weight_new = finish(now, right, right_o, colsq, ortho, weight)
    return (momentum_new, weight_new, basis_new)


def solution(mesh):
    placed = (P(F, T), P(F, T), P(F, T), P(T, None))
    return jax.shard_map(
        local,
        mesh=mesh,
        in_specs=placed,
        out_specs=(P(F, T), P(F, T), P(T, None)),
        check_vma=False,
    )
```
